32 devices in a mesh: mem: 8 (over z, core), tensor: 4 (over y, x).
Axes of the slice: x: 2, y: 2, z: 4, core: 2. Of those that a mesh axis runs over, the one named last changes fastest.
Arguments:
- tokens: bfloat16 [4096, 4096], P('mem', 'tensor'), may hold values from -6 to 6
- neighbours: int32 [64, 2, 2], replicated, may hold values from 0 to 63, as said below
- memory_bank: bfloat16 [512, 128, 896], P('mem', 'tensor'), may hold values from -340 to 340
- w_query: bfloat16 [4096, 4096], P(None, 'tensor'), may hold values from -0.09375 to 0.09375
- w_key: bfloat16 [896, 4096], P(None, 'tensor'), may hold values from -0.1875 to 0.1875
- w_value: bfloat16 [896, 4096], P(None, 'tensor'), may hold values from -0.1875 to 0.1875
- w_out: bfloat16 [4096, 4096], P('tensor', 'mem'), may hold values from -0.09375 to 0.09375
Outputs:
- mixed: bfloat16 [4096, 4096], P('mem', 'tensor')
The draws below stay inside these ranges and needn't reach their ends.
Inputs may be any that keep to these rules, and one draw needn't show every extreme that they name: `neighbours`: among the 16 entries of the spans c with c // 8 equal to one value, no memory shard is named more than 2 times; some shard is named exactly 2 times for every such value.
All inputs are finite; a program needn't handle non-finite values.
Results may differ from the reference program's by a relative error of at most 0.014.
The reference program's roundings to bfloat16 on the way count: a program that leaves them out, or rounds other values in their place, can miss the bound.
Values may be sent and summed in bfloat16 or wider, within the bound.
A program may use at most 64 MiB of HBM per device.

```python
import math
import jax
import jax.numpy as jnp
from jax import lax

D = 4096
HEADS = 32
DH = 128
ENC = 896
SPAN = 64
NB = 2
NLEN = 128
TOK_GROUP = 512
ROWS_DEV = 64
HD = 4096
HEAD_BLOCK = 8
GROUP_SPANS = 8
CAP = 2
SPANS = 64
TOKENS = 4096
BANK_ROWS = 512
N_MEM = 8
N_TENSOR = 4


def draw_neighbours(key, part):
    requests = NB * GROUP_SPANS
    others = CAP * (N_MEM - 1)
    hot_key, group_key, row_key = jax.random.split(key, 3)
    hot_shard = jax.random.randint(hot_key, (), 0, N_MEM)

    def one_group(group_seed):
        pick_key, order_key = jax.random.split(group_seed)
        offsets = jnp.arange(others, dtype=jnp.int32) // CAP + 1
        picked = jax.random.permutation(pick_key, others)[:requests - CAP]
        owner_list = jnp.concatenate([jnp.zeros((CAP,), jnp.int32), offsets[picked]])
        owner_list = (owner_list + hot_shard) % N_MEM
        shuffle = jax.random.permutation(order_key, requests)
        return (owner_list[shuffle], shuffle)
    group_seeds = jax.random.split(group_key, N_MEM)
    owner_table, shuffles = jax.vmap(one_group)(group_seeds)
    row_table = jax.random.randint(row_key, (N_MEM, requests), 0, ROWS_DEV)
    first_rows = jnp.where(shuffles[0] == 0, ROWS_DEV - 1, jnp.where(shuffles[0] == 1, 0, row_table[0]))
    row_table = row_table.at[0].set(first_rows)
    result = jnp.stack([owner_table, row_table], axis=-1).reshape(SPANS, NB, 2)
    return result.astype(jnp.int32)


def draw_memory_bank(key, part):
    base_key = jax.random.fold_in(key, 0)
    shape = (BANK_ROWS, NLEN, ENC)
    bank = jnp.clip(jax.random.normal(base_key, shape, jnp.float32), -6.0, 6.0)
    return bank.astype(jnp.bfloat16)


def steps_of(key, shape, pieces, low, high):
    def one(dim, blocks):
        heights = jax.random.uniform(jax.random.fold_in(jax.random.fold_in(key, 6), dim), (blocks,), jnp.float32, low / len(pieces), high / len(pieces))
        return jnp.repeat(jnp.exp(heights), shape[dim] // blocks).reshape((-1,) + (1,) * (len(shape) - dim - 1))

    factor_of = one(*pieces[0])
    for cut in pieces[1:]:
        factor_of = factor_of * one(*cut)
    return factor_of


def normal_values(own_key, extent, deviation, limit, cuts=(), held_as=jnp.bfloat16):
    level = steps_of(own_key, extent, cuts, -0.22, 0.18) if cuts else 1.0
    array = jax.random.normal(own_key, extent, jnp.float32) * deviation * level
    return jnp.minimum(jnp.maximum(array, -limit), limit).astype(held_as)


def setup_inputs(seed: int = 0) -> dict:
    key_of = jax.random.split(jax.random.key(seed), 8)
    tokens = normal_values(key_of[0], (TOKENS, D), 1.0, 6.0, ((0, 8), (1, 4)))
    neighbours = draw_neighbours(jax.random.fold_in(key_of[7], 71), 0)
    memory_bank = draw_memory_bank(jax.random.fold_in(key_of[7], 71), 0)
    w_query = normal_values(key_of[3], (D, HD), D ** -0.5, 0.09375, ((1, 4),))
    w_key = normal_values(key_of[4], (ENC, HD), ENC ** -0.5, 0.1875, ((1, 4),))
    w_value = normal_values(key_of[5], (ENC, HD), ENC ** -0.5, 0.1875, ((1, 4),))
    w_out = normal_values(key_of[6], (HD, D), HD ** -0.5, 0.09375, ((0, 4), (1, 8)))
    return dict(tokens=tokens, neighbours=neighbours, memory_bank=memory_bank, w_query=w_query, w_key=w_key, w_value=w_value, w_out=w_out)


def reference(tokens, neighbours, memory_bank, w_query, w_key, w_value, w_out):
    group_len = TOK_GROUP
    requests = NB * GROUP_SPANS
    block_cols = HEAD_BLOCK * DH
    score_scale = 1.0 / math.sqrt(DH)

    def one_group(group):
        rows_here = lax.dynamic_slice_in_dim(tokens, group * group_len, group_len, 0)
        listing = lax.dynamic_slice_in_dim(neighbours, group * GROUP_SPANS, GROUP_SPANS, 0).reshape(requests, 2)
        flat_ids = (listing[:, 0] * ROWS_DEV + listing[:, 1]).astype(jnp.int32)
        encoded = jnp.take(memory_bank, flat_ids, axis=0).reshape(requests * NLEN, ENC)
        queries = (jnp.dot(rows_here, w_query, preferred_element_type=jnp.float32) * score_scale).astype(jnp.bfloat16)
        key_rows = jnp.dot(encoded, w_key, preferred_element_type=jnp.float32).astype(jnp.bfloat16)
        value_rows = jnp.dot(encoded, w_value, preferred_element_type=jnp.float32).astype(jnp.bfloat16)
        query_block = queries.astype(jnp.float32).reshape(GROUP_SPANS, SPAN, HEADS, DH)
        key_block = key_rows.astype(jnp.float32).reshape(GROUP_SPANS, NB * NLEN, HEADS, DH)
        value_block = value_rows.astype(jnp.float32).reshape(GROUP_SPANS, NB * NLEN, HEADS, DH)
        scores = jnp.einsum('cqhd,ckhd->chqk', query_block, key_block)
        row_max = lax.optimization_barrier(jnp.max(scores, axis=-1, keepdims=True))
        lifted = jnp.exp(scores - row_max)
        normed = lifted / lax.optimization_barrier(jnp.sum(lifted, axis=-1, keepdims=True))
        weights = normed.astype(jnp.bfloat16)
        attended = jnp.einsum('chqk,ckhd->cqhd', weights.astype(jnp.float32), value_block)
        attended = attended.astype(jnp.bfloat16).reshape(group_len, HD)
        attended_blocks = attended.astype(jnp.float32).reshape(group_len, N_TENSOR, block_cols)
        out_blocks = w_out.astype(jnp.float32).reshape(N_TENSOR, block_cols, D)
        partial_value = jnp.einsum('gtk,tkd->tgd', attended_blocks, out_blocks).astype(jnp.bfloat16)
        partial_value = lax.optimization_barrier(partial_value)
        return lax.optimization_barrier(jnp.sum(partial_value.astype(jnp.float32), axis=0)).astype(jnp.bfloat16)
    mixed = lax.map(one_group, jnp.arange(N_MEM, dtype=jnp.int32))
    return mixed.reshape(TOKENS, D)
```

```python
import functools
import math

import jax
import jax.numpy as jnp
from jax import lax
from jax.experimental import pallas as pl
from jax.experimental.pallas import tpu as pltpu
from jax.sharding import PartitionSpec as P

DH = 128
NB = 2


def body(tokens, neighbours, memory_bank, w_query, w_key, w_value, w_out):
    mem_count = lax.axis_size("mem")
    mem_index = lax.axis_index("mem")
    slice_len = memory_bank.shape[1]
    enc_width = memory_bank.shape[2]
    head_cols = w_query.shape[1]
    heads_here = head_cols // DH
    requests = neighbours.shape[0] * neighbours.shape[1] // mem_count
    spans_here = requests // NB
    slot_count = max(2, (requests + mem_count - 1) // mem_count)
    score_scale = 1.0 / math.sqrt(DH)
    query_sum = jnp.dot(
        lax.all_gather(tokens, "tensor", axis=1, tiled=True),
        w_query,
        preferred_element_type=jnp.float32,
    )
    queries = (query_sum * score_scale).astype(jnp.bfloat16)
    listing = neighbours.reshape(mem_count, requests, 2)
    owner_ids = listing[:, :, 0]
    row_ids = listing[:, :, 1]
    owned_here = owner_ids == mem_index
    slot_rank = jnp.cumsum(owned_here.astype(jnp.int32), axis=1) - 1
    slot_ids = jnp.arange(slot_count, dtype=jnp.int32)
    chosen = owned_here[:, None, :] & (slot_rank[:, None, :] == slot_ids[None, :, None])
    wanted = jnp.sum(jnp.where(chosen, row_ids[:, None, :], 0), axis=2)
    outgoing = jnp.take(memory_bank, wanted.reshape(-1), axis=0).reshape(
        mem_count, slot_count, slice_len, enc_width
    )
    incoming = lax.all_to_all(outgoing, "mem", split_axis=0, concat_axis=0, tiled=True)
    own_list = lax.dynamic_index_in_dim(listing, mem_index, 0, keepdims=False)
    own_owner = own_list[:, 0]
    positions = jnp.arange(requests, dtype=jnp.int32)
    earlier = positions[None, :] < positions[:, None]
    same_owner = own_owner[:, None] == own_owner[None, :]
    own_rank = jnp.sum((same_owner & earlier).astype(jnp.int32), axis=1)
    source = own_owner * slot_count + own_rank
    fetched = jnp.take(
        incoming.reshape(mem_count * slot_count, slice_len, enc_width), source, axis=0
    )
    joined = jnp.concatenate([w_key, w_value], axis=1)
    key_value = jnp.dot(
        lax.all_gather(fetched, "tensor", axis=1, tiled=True),
        joined,
        preferred_element_type=jnp.float32,
    ).astype(jnp.bfloat16)
    bank_len = key_value.shape[1]
    key_block = key_value[:, :, :head_cols].reshape(spans_here, NB * bank_len, heads_here, DH)
    value_block = key_value[:, :, head_cols:].reshape(spans_here, NB * bank_len, heads_here, DH)
    query_block = queries.reshape(spans_here, -1, heads_here, DH)
    scores = jnp.einsum(
        "cqhd,ckhd->chqk", query_block, key_block, preferred_element_type=jnp.float32
    )
    row_max = jnp.max(scores, axis=-1, keepdims=True)
    lifted = jnp.exp(scores - row_max)
    normed = lifted / jnp.sum(lifted, axis=-1, keepdims=True)
    weights = normed.astype(jnp.bfloat16)
    attended = jnp.einsum(
        "chqk,ckhd->cqhd", weights, value_block, preferred_element_type=jnp.float32
    )
    attended = attended.astype(jnp.bfloat16).reshape(-1, head_cols)
    partial_value = jnp.dot(
        attended,
        lax.all_gather(w_out, "mem", axis=1, tiled=True),
        preferred_element_type=jnp.float32,
    )
    summed = lax.psum_scatter(
        partial_value.astype(jnp.bfloat16), "tensor", scatter_dimension=1, tiled=True
    )
    return summed


MESH = pl.DeviceIdType.MESH


def fused_kernel(
    mem_count, tensor_count, spans, score_scale,
    source, tokens, outgoing, w_query, w_key, w_value, w_out, result,
    tok, wq, wk, wv, enc, keys, values, acc, queries, attended, wo,
    part_d, part_x, part_y, relay_x, relay_y, got_x, got_y,
    load_sem, tok_send, tok_recv, bank_send, bank_recv, near_send, near_recv,
    wo_send, wo_recv, core_send, core_recv, red_send, red_recv,
):
    me = lax.axis_index("mem")
    t = lax.axis_index("tensor")
    tx = t + 1 - 2 * (t % 2)
    ty = (t + 2) % 4
    td = (tx + 2) % 4
    z_count = mem_count // 2
    z = me // 2
    core = me % 2
    mate = me + 1 - 2 * core
    rows = tok.shape[1]
    half = rows // 2
    width = tok.shape[2]
    tile = 256

    def remote(src, dst, send, recv, **where):
        return pltpu.make_async_remote_copy(
            src_ref=src, dst_ref=dst, send_sem=send, recv_sem=recv,
            device_id=where, device_id_type=MESH,
        )

    def arrived(ref, send, recv):
        remote(ref, ref, send, recv, tensor=tx).wait_recv()

    def left(ref, send, recv):
        remote(ref, ref, send, recv, tensor=tx).wait_send()

    barrier = pltpu.get_barrier_semaphore()
    for d in range(1, mem_count):
        pl.semaphore_signal(barrier, inc=1, device_id={"mem": (me + d) % mem_count}, device_id_type=MESH)
    for other in (tx, ty):
        pl.semaphore_signal(barrier, inc=1, device_id={"tensor": other}, device_id_type=MESH)

    loads = [
        pltpu.make_async_copy(tokens, tok.at[t], load_sem.at[0]),
        pltpu.make_async_copy(outgoing.at[me], enc.at[t, me], load_sem.at[1]),
        pltpu.make_async_copy(w_key, wk, load_sem.at[2]),
        pltpu.make_async_copy(w_value, wv, load_sem.at[3]),
        pltpu.make_async_copy(w_out, wo.at[me], load_sem.at[4]),
    ]
    wq_loads = []
    for i, b in enumerate((t, tx, ty, td)):
        wq_loads.append(pltpu.make_async_copy(w_query.at[b], wq.at[b], load_sem.at[5 + i]))
    for copy in loads[:2] + wq_loads + loads[2:]:
        copy.start()
    pl.semaphore_wait(barrier, mem_count + 1)

    bank_copies = []
    for d in range(1, mem_count):
        to = (me + d) % mem_count
        copy = remote(outgoing.at[to], enc.at[t, me], bank_send.at[d], bank_recv.at[me], mem=to)
        copy.start()
        bank_copies.append(copy)

    tok_copies = []
    for c in range(2):
        part = pl.ds(c * half, half)
        for n, other in enumerate((tx, ty)):
            copy = remote(
                tokens.at[part], tok.at[t, part], tok_send.at[2 * n + c], tok_recv.at[2 * n + c], tensor=other
            )
            copy.start()
            tok_copies.append(copy)

    @pl.when(z < z_count - 1)
    def _():
        remote(w_out, wo.at[me], wo_send.at[0, 0], wo_recv.at[0, 1], mem=me + 2).start()

    @pl.when(z > 0)
    def _():
        remote(w_out, wo.at[me], wo_send.at[1, 0], wo_recv.at[1, 1], mem=me - 2).start()

    remote(w_out, wo.at[me], core_send.at[z], core_recv.at[z], mem=mate).start()

    def pass_on(s):
        @pl.when(z >= s)
        def _():
            ref = wo.at[me - 2 * s]
            arrived(ref, wo_send.at[0, s], wo_recv.at[0, s])
            remote(ref, ref, core_send.at[z - s], core_recv.at[z - s], mem=mate).start()
            if s < z_count - 1:
                @pl.when(z < z_count - 1)
                def _():
                    remote(ref, ref, wo_send.at[0, s], wo_recv.at[0, s + 1], mem=me + 2).start()

        @pl.when(z + s < z_count)
        def _():
            ref = wo.at[me + 2 * s]
            arrived(ref, wo_send.at[1, s], wo_recv.at[1, s])
            remote(ref, ref, core_send.at[z + s], core_recv.at[z + s], mem=mate).start()
            if s < z_count - 1:
                @pl.when(z > 0)
                def _():
                    remote(ref, ref, wo_send.at[1, s], wo_recv.at[1, s + 1], mem=me - 2).start()

    def add_queries(b, first):
        @pl.loop(0, width // tile)
        def _(n):
            cols = pl.ds(pl.multiple_of(n * tile, tile), tile)
            term = jnp.dot(tok[b], wq[b, :, cols], preferred_element_type=jnp.float32)
            if first:
                acc[:, cols] = term
            else:
                acc[:, cols] += term

    enc_rows = enc.shape[1] * enc.shape[2]
    enc_width = enc.shape[3]
    slots = keys.shape[1]
    length = keys.shape[2]

    def make_kv(b):
        @pl.loop(0, width // tile)
        def _(n):
            cols = pl.ds(pl.multiple_of(n * tile, tile), tile)
            block = enc[b].reshape(enc_rows, enc_width)
            k = jnp.dot(block, wk[:, cols], preferred_element_type=jnp.float32)
            keys[b, :, :, cols] = k.astype(jnp.bfloat16).reshape(slots, length, tile)
            v = jnp.dot(block, wv[:, cols], preferred_element_type=jnp.float32)
            values[b, :, :, cols] = v.astype(jnp.bfloat16).reshape(slots, length, tile)

    loads[0].wait()
    wq_loads[0].wait()
    add_queries(t, True)

    near_copies = []
    loads[1].wait()
    order = [0] + [d for k in range(1, mem_count // 2 + 1) for d in sorted({k, mem_count - k})]
    for d in order:
        frm = (me + d) % mem_count
        ref = enc.at[t, frm]
        if d:
            arrived(ref, bank_send.at[0], bank_recv.at[frm])
        for n, other in enumerate((tx, ty)):
            copy = remote(ref, ref, near_send.at[n, frm], near_recv.at[n, frm], tensor=other)
            copy.start()
            near_copies.append(copy)

    for c, b, other in ((0, tx, ty), (1, ty, tx)):
        ref = tok.at[b, pl.ds(c * half, half)]
        arrived(ref, tok_send.at[4 + c], tok_recv.at[2 * c + c])
        copy = remote(ref, ref, tok_send.at[4 + c], tok_recv.at[4 + c], tensor=other)
        copy.start()
        tok_copies.append(copy)

    pass_on(1)
    loads[2].wait()
    loads[3].wait()
    make_kv(t)
    arrived(tok.at[tx, pl.ds(half, half)], tok_send.at[0], tok_recv.at[1])
    wq_loads[1].wait()
    add_queries(tx, False)
    arrived(tok.at[ty, pl.ds(0, half)], tok_send.at[0], tok_recv.at[2])
    wq_loads[2].wait()
    add_queries(ty, False)

    for i in range(0, mem_count, 2):
        for n, b, other in ((0, tx, ty), (1, ty, tx)):
            ref = enc.at[b, i + n]
            arrived(ref, near_send.at[2, i + n], near_recv.at[n, i + n])
            copy = remote(ref, ref, near_send.at[2, i + n], near_recv.at[2, i + n], tensor=other)
            copy.start()
            near_copies.append(copy)
    if z_count > 2:
        pass_on(2)
    for i in range(1, mem_count, 2):
        arrived(enc.at[tx, i], near_send.at[0, 0], near_recv.at[0, i])
    make_kv(tx)
    for i in range(0, mem_count, 2):
        arrived(enc.at[ty, i], near_send.at[0, 0], near_recv.at[1, i])
    make_kv(ty)
    arrived(tok.at[td, pl.ds(0, half)], tok_send.at[0], tok_recv.at[4])
    arrived(tok.at[td, pl.ds(half, half)], tok_send.at[0], tok_recv.at[5])
    wq_loads[3].wait()
    add_queries(td, False)
    queries[...] = (acc[...] * score_scale).astype(jnp.bfloat16)
    for i in range(mem_count):
        arrived(enc.at[td, i], near_send.at[0, 0], near_recv.at[2, i])
    make_kv(td)

    span_rows = rows // spans

    @pl.loop(0, spans)
    def _(c):
        first = source[NB * c]
        second = source[NB * c + 1]
        where = pl.ds(pl.multiple_of(c * span_rows, span_rows), span_rows)
        for h in range(width // DH):
            cols = slice(h * DH, (h + 1) * DH)
            k = jnp.concatenate(
                [keys[b, s, :, cols] for s in (first, second) for b in range(tensor_count)], axis=0
            )
            v = jnp.concatenate(
                [values[b, s, :, cols] for s in (first, second) for b in range(tensor_count)], axis=0
            )
            scores = lax.dot_general(
                queries[where, cols], k, (((1,), (1,)), ((), ())), preferred_element_type=jnp.float32
            )
            lifted = jnp.exp(scores - jnp.max(scores, axis=-1, keepdims=True))
            weights = (lifted * (1.0 / jnp.sum(lifted, axis=-1, keepdims=True))).astype(jnp.bfloat16)
            attended[where, cols] = jnp.dot(weights, v, preferred_element_type=jnp.float32).astype(jnp.bfloat16)

    for s in range(3, z_count):
        pass_on(s)
    loads[4].wait()
    for i in range(z_count):
        arrived(wo.at[2 * i + 1 - core], core_send.at[0], core_recv.at[i])

    per = mem_count // tensor_count
    wide = wo.shape[2]

    def project(b, lo, out, extra=None, at=0):
        @pl.loop(0, per)
        def _(j):
            @pl.loop(0, wide // tile)
            def _(n):
                inner = pl.ds(pl.multiple_of(n * tile, tile), tile)
                outer = pl.ds(pl.multiple_of(j * wide + n * tile, tile), tile)
                term = jnp.dot(
                    attended[lo : lo + half], wo[b * per + j, :, inner], preferred_element_type=jnp.float32
                ).astype(jnp.bfloat16)
                if extra is not None:
                    term = (term.astype(jnp.float32) + extra[:, outer].astype(jnp.float32)).astype(jnp.bfloat16)
                out[lo : lo + half, outer] = term

    red_copies = []

    def give(ref, dst, i, other):
        copy = remote(ref, dst, red_send.at[i], red_recv.at[i], tensor=other)
        copy.start()
        red_copies.append(copy)

    low, high = pl.ds(0, half), pl.ds(half, half)
    project(td, 0, part_d)
    give(part_d.at[low], relay_x, 0, tx)
    project(td, half, part_d)
    give(part_d.at[high], relay_y, 1, ty)
    project(tx, 0, part_x)
    give(part_x.at[low], got_x.at[low], 2, tx)
    project(ty, half, part_y)
    give(part_y.at[high], got_y.at[high], 3, ty)
    arrived(relay_x, red_send.at[0], red_recv.at[0])
    project(ty, 0, part_y, relay_x)
    give(part_y.at[low], got_y.at[low], 4, ty)
    arrived(relay_y, red_send.at[0], red_recv.at[1])
    project(tx, half, part_x, relay_y)
    give(part_x.at[high], got_x.at[high], 5, tx)
    red_copies[0].wait_send()
    red_copies[1].wait_send()
    project(t, 0, part_d)
    project(t, half, part_d)
    for i, ref in ((2, got_x.at[low]), (3, got_y.at[high]), (4, got_y.at[low]), (5, got_x.at[high])):
        arrived(ref, red_send.at[0], red_recv.at[i])
    result[...] = (
        part_d[...].astype(jnp.float32) + got_x[...].astype(jnp.float32) + got_y[...].astype(jnp.float32)
    ).astype(jnp.bfloat16)

    for copy in bank_copies + tok_copies + near_copies + red_copies[2:]:
        copy.wait_send()
    for s in range(z_count - 1):
        @pl.when((z < z_count - 1) & (z >= s))
        def _():
            left(wo.at[0], wo_send.at[0, s], wo_recv.at[0, 0])

        @pl.when((z > 0) & (z + s < z_count))
        def _():
            left(wo.at[0], wo_send.at[1, s], wo_recv.at[0, 0])
    for i in range(z_count):
        left(wo.at[0], core_send.at[i], core_recv.at[0])


def fused_body(tokens, neighbours, memory_bank, w_query, w_key, w_value, w_out):
    mem_count = lax.axis_size("mem")
    tensor_count = lax.axis_size("tensor")
    mem_index = lax.axis_index("mem")
    slice_len, enc_width = memory_bank.shape[1:]
    requests = neighbours.shape[0] * neighbours.shape[1] // mem_count
    spans = requests // NB
    slot_count = requests // mem_count
    rows, width = tokens.shape
    listing = neighbours.reshape(mem_count, requests, 2)
    owner_ids = listing[:, :, 0]
    row_ids = listing[:, :, 1]
    owned_here = owner_ids == mem_index
    slot_rank = jnp.cumsum(owned_here.astype(jnp.int32), axis=1) - 1
    slot_ids = jnp.arange(slot_count, dtype=jnp.int32)
    chosen = owned_here[:, None, :] & (slot_rank[:, None, :] == slot_ids[None, :, None])
    wanted = jnp.sum(jnp.where(chosen, row_ids[:, None, :], 0), axis=2)
    outgoing = jnp.take(memory_bank, wanted.reshape(-1), axis=0, mode="clip").reshape(
        mem_count, slot_count * slice_len, enc_width
    )
    own_owner = lax.dynamic_index_in_dim(listing, mem_index, 0, keepdims=False)[:, 0]
    positions = jnp.arange(requests, dtype=jnp.int32)
    earlier = positions[None, :] < positions[:, None]
    same_owner = own_owner[:, None] == own_owner[None, :]
    own_rank = jnp.sum((same_owner & earlier).astype(jnp.int32), axis=1)
    source = own_owner * slot_count + own_rank
    z_count = mem_count // 2
    bf16 = jnp.bfloat16
    half = rows // 2
    slots = mem_count * slot_count
    hbm = pl.BlockSpec(memory_space=pl.ANY)
    dma = pltpu.SemaphoreType.DMA
    return pl.pallas_call(
        functools.partial(fused_kernel, mem_count, tensor_count, spans, 1.0 / math.sqrt(DH)),
        out_shape=jax.ShapeDtypeStruct((rows, width), bf16),
        in_specs=[pl.BlockSpec(memory_space=pltpu.SMEM)] + [hbm] * 6,
        out_specs=pl.BlockSpec(memory_space=pltpu.VMEM),
        scratch_shapes=[
            pltpu.VMEM((tensor_count, rows, width), bf16),
            pltpu.VMEM((tensor_count, width, width), bf16),
            pltpu.VMEM((enc_width, width), bf16),
            pltpu.VMEM((enc_width, width), bf16),
            pltpu.VMEM((tensor_count, mem_count, slot_count * slice_len, enc_width), bf16),
            pltpu.VMEM((tensor_count, slots, slice_len, width), bf16),
            pltpu.VMEM((tensor_count, slots, slice_len, width), bf16),
            pltpu.VMEM((rows, width), jnp.float32),
            pltpu.VMEM((rows, width), bf16),
            pltpu.VMEM((rows, width), bf16),
            pltpu.VMEM((mem_count,) + w_out.shape, bf16),
            pltpu.VMEM((rows, width), bf16),
            pltpu.VMEM((rows, width), bf16),
            pltpu.VMEM((rows, width), bf16),
            pltpu.VMEM((half, width), bf16),
            pltpu.VMEM((half, width), bf16),
            pltpu.VMEM((rows, width), bf16),
            pltpu.VMEM((rows, width), bf16),
            dma((9,)),
            dma((6,)),
            dma((6,)),
            dma((mem_count,)),
            dma((mem_count,)),
            dma((3, mem_count)),
            dma((3, mem_count)),
            dma((2, z_count)),
            dma((2, z_count)),
            dma((z_count,)),
            dma((z_count,)),
            dma((6,)),
            dma((6,)),
        ],
        compiler_params=pltpu.CompilerParams(
            collective_id=0, has_side_effects=True, vmem_limit_bytes=58 * 1024 * 1024
        ),
    )(source, tokens, outgoing, w_query.reshape(tensor_count, width, width), w_key, w_value, w_out)


def fits(mesh, tokens, neighbours, memory_bank, w_query):
    mem_count, tensor_count = mesh.shape["mem"], mesh.shape["tensor"]
    requests = neighbours.shape[0] * neighbours.shape[1] // mem_count
    return (
        tensor_count == 4
        and mem_count % tensor_count == 0
        and requests == NB * mem_count
        and tokens.shape[1] == w_query.shape[1]
    )


def solution(mesh):
    def run(*args):
        chosen = fused_body if fits(mesh, *args[:4]) else body
        return jax.shard_map(
            chosen,
            mesh=mesh,
            in_specs=(
                P("mem", "tensor"),
                P(),
                P("mem", "tensor", None),
                P(None, "tensor"),
                P(None, "tensor"),
                P(None, "tensor"),
                P("tensor", "mem"),
            ),
            out_specs=P("mem", "tensor"),
            check_vma=False,
        )(*args)

    return run
```

```python
import functools
import math

import jax
import jax.numpy as jnp
from jax import lax
from jax.experimental import pallas as pl
from jax.experimental.pallas import tpu as pltpu
from jax.sharding import PartitionSpec as P

DH = 128
NB = 2


def body(tokens, neighbours, memory_bank, w_query, w_key, w_value, w_out):
    mem_count = lax.axis_size("mem")
    mem_index = lax.axis_index("mem")
    slice_len = memory_bank.shape[1]
    enc_width = memory_bank.shape[2]
    head_cols = w_query.shape[1]
    heads_here = head_cols // DH
    requests = neighbours.shape[0] * neighbours.shape[1] // mem_count
    spans_here = requests // NB
    slot_count = max(2, (requests + mem_count - 1) // mem_count)
    score_scale = 1.0 / math.sqrt(DH)
    query_sum = jnp.dot(
        lax.all_gather(tokens, "tensor", axis=1, tiled=True),
        w_query,
        preferred_element_type=jnp.float32,
    )
    queries = (query_sum * score_scale).astype(jnp.bfloat16)
    listing = neighbours.reshape(mem_count, requests, 2)
    owner_ids = listing[:, :, 0]
    row_ids = listing[:, :, 1]
    owned_here = owner_ids == mem_index
    slot_rank = jnp.cumsum(owned_here.astype(jnp.int32), axis=1) - 1
    slot_ids = jnp.arange(slot_count, dtype=jnp.int32)
    chosen = owned_here[:, None, :] & (slot_rank[:, None, :] == slot_ids[None, :, None])
    wanted = jnp.sum(jnp.where(chosen, row_ids[:, None, :], 0), axis=2)
    outgoing = jnp.take(memory_bank, wanted.reshape(-1), axis=0).reshape(
        mem_count, slot_count, slice_len, enc_width
    )
    incoming = lax.all_to_all(outgoing, "mem", split_axis=0, concat_axis=0, tiled=True)
    own_list = lax.dynamic_index_in_dim(listing, mem_index, 0, keepdims=False)
    own_owner = own_list[:, 0]
    positions = jnp.arange(requests, dtype=jnp.int32)
    earlier = positions[None, :] < positions[:, None]
    same_owner = own_owner[:, None] == own_owner[None, :]
    own_rank = jnp.sum((same_owner & earlier).astype(jnp.int32), axis=1)
    source = own_owner * slot_count + own_rank
    fetched = jnp.take(
        incoming.reshape(mem_count * slot_count, slice_len, enc_width), source, axis=0
    )
    joined = jnp.concatenate([w_key, w_value], axis=1)
    key_value = jnp.dot(
        lax.all_gather(fetched, "tensor", axis=1, tiled=True),
        joined,
        preferred_element_type=jnp.float32,
    ).astype(jnp.bfloat16)
    bank_len = key_value.shape[1]
    key_block = key_value[:, :, :head_cols].reshape(spans_here, NB * bank_len, heads_here, DH)
    value_block = key_value[:, :, head_cols:].reshape(spans_here, NB * bank_len, heads_here, DH)
    query_block = queries.reshape(spans_here, -1, heads_here, DH)
    scores = jnp.einsum(
        "cqhd,ckhd->chqk", query_block, key_block, preferred_element_type=jnp.float32
    )
    row_max = jnp.max(scores, axis=-1, keepdims=True)
    lifted = jnp.exp(scores - row_max)
    normed = lifted / jnp.sum(lifted, axis=-1, keepdims=True)
    weights = normed.astype(jnp.bfloat16)
    attended = jnp.einsum(
        "chqk,ckhd->cqhd", weights, value_block, preferred_element_type=jnp.float32
    )
    attended = attended.astype(jnp.bfloat16).reshape(-1, head_cols)
    partial_value = jnp.dot(
        attended,
        lax.all_gather(w_out, "mem", axis=1, tiled=True),
        preferred_element_type=jnp.float32,
    )
    summed = lax.psum_scatter(
        partial_value.astype(jnp.bfloat16), "tensor", scatter_dimension=1, tiled=True
    )
    return summed


MESH = pl.DeviceIdType.MESH


def fused_kernel(
    mem_count, tensor_count, spans, score_scale,
    source, tokens, outgoing, w_query, w_key, w_value, w_out, result,
    tok, wq, wk, wv, enc, keys, values, acc, queries, attended, wo,
    part_d, part_x, part_y, relay_x, relay_y, got_x, got_y,
    load_sem, tok_send, tok_recv, bank_send, bank_recv, near_send, near_recv,
    wo_send, wo_recv, core_send, core_recv, red_send, red_recv,
):
    me = lax.axis_index("mem")
    t = lax.axis_index("tensor")
    tx = t + 1 - 2 * (t % 2)
    ty = (t + 2) % 4
    td = (tx + 2) % 4
    z_count = mem_count // 2
    z = me // 2
    core = me % 2
    mate = me + 1 - 2 * core
    rows = tok.shape[1]
    half = rows // 2
    width = tok.shape[2]
    tile = 256

    def remote(src, dst, send, recv, **where):
        return pltpu.make_async_remote_copy(
            src_ref=src, dst_ref=dst, send_sem=send, recv_sem=recv,
            device_id=where, device_id_type=MESH,
        )

    def arrived(ref, send, recv):
        remote(ref, ref, send, recv, tensor=tx).wait_recv()

    def left(ref, send, recv):
        remote(ref, ref, send, recv, tensor=tx).wait_send()

    barrier = pltpu.get_barrier_semaphore()
    for d in range(1, mem_count):
        pl.semaphore_signal(barrier, inc=1, device_id={"mem": (me + d) % mem_count}, device_id_type=MESH)
    for other in (tx, ty):
        pl.semaphore_signal(barrier, inc=1, device_id={"tensor": other}, device_id_type=MESH)

    loads = [
        pltpu.make_async_copy(tokens, tok.at[t], load_sem.at[0]),
        pltpu.make_async_copy(outgoing.at[me], enc.at[t, me], load_sem.at[1]),
        pltpu.make_async_copy(w_key, wk, load_sem.at[2]),
        pltpu.make_async_copy(w_value, wv, load_sem.at[3]),
        pltpu.make_async_copy(w_out, wo.at[me], load_sem.at[4]),
    ]
    wq_loads = []
    for i, b in enumerate((t, tx, ty, td)):
        wq_loads.append(pltpu.make_async_copy(w_query.at[b], wq.at[b], load_sem.at[5 + i]))
    for copy in loads[:2] + wq_loads + loads[2:]:
        copy.start()
    pl.semaphore_wait(barrier, mem_count + 1)

    bank_copies = []
    for d in range(1, mem_count):
        to = (me + d) % mem_count
        copy = remote(outgoing.at[to], enc.at[t, me], bank_send.at[d], bank_recv.at[me], mem=to)
        copy.start()
        bank_copies.append(copy)

    tok_copies = []
    for c in range(2):
        part = pl.ds(c * half, half)
        for n, other in enumerate((tx, ty)):
            copy = remote(
                tokens.at[part], tok.at[t, part], tok_send.at[2 * n + c], tok_recv.at[2 * n + c], tensor=other
            )
            copy.start()
            tok_copies.append(copy)

    @pl.when(z < z_count - 1)
    def _():
        remote(w_out, wo.at[me], wo_send.at[0, 0], wo_recv.at[0, 1], mem=me + 2).start()

    @pl.when(z > 0)
    def _():
        remote(w_out, wo.at[me], wo_send.at[1, 0], wo_recv.at[1, 1], mem=me - 2).start()

    remote(w_out, wo.at[me], core_send.at[z], core_recv.at[z], mem=mate).start()

    def pass_on(s):
        @pl.when(z >= s)
        def _():
            ref = wo.at[me - 2 * s]
            arrived(ref, wo_send.at[0, s], wo_recv.at[0, s])
            remote(ref, ref, core_send.at[z - s], core_recv.at[z - s], mem=mate).start()
            if s < z_count - 1:
                @pl.when(z < z_count - 1)
                def _():
                    remote(ref, ref, wo_send.at[0, s], wo_recv.at[0, s + 1], mem=me + 2).start()

        @pl.when(z + s < z_count)
        def _():
            ref = wo.at[me + 2 * s]
            arrived(ref, wo_send.at[1, s], wo_recv.at[1, s])
            remote(ref, ref, core_send.at[z + s], core_recv.at[z + s], mem=mate).start()
            if s < z_count - 1:
                @pl.when(z > 0)
                def _():
                    remote(ref, ref, wo_send.at[1, s], wo_recv.at[1, s + 1], mem=me - 2).start()

    def add_queries(b, first):
        @pl.loop(0, width // tile)
        def _(n):
            cols = pl.ds(pl.multiple_of(n * tile, tile), tile)
            term = jnp.dot(tok[b], wq[b, :, cols], preferred_element_type=jnp.float32)
            if first:
                acc[:, cols] = term
            else:
                acc[:, cols] += term

    enc_rows = enc.shape[1] * enc.shape[2]
    enc_width = enc.shape[3]
    slots = keys.shape[1]
    length = keys.shape[2]

    def make_kv(b):
        @pl.loop(0, width // tile)
        def _(n):
            cols = pl.ds(pl.multiple_of(n * tile, tile), tile)
            block = enc[b].reshape(enc_rows, enc_width)
            k = jnp.dot(block, wk[:, cols], preferred_element_type=jnp.float32)
            keys[b, :, :, cols] = k.astype(jnp.bfloat16).reshape(slots, length, tile)
            v = jnp.dot(block, wv[:, cols], preferred_element_type=jnp.float32)
            values[b, :, :, cols] = v.astype(jnp.bfloat16).reshape(slots, length, tile)

    loads[0].wait()
    wq_loads[0].wait()
    add_queries(t, True)

    near_copies = []
    loads[1].wait()
    order = [0] + [d for k in range(1, mem_count // 2 + 1) for d in sorted({k, mem_count - k})]
    for d in order:
        frm = (me + d) % mem_count
        ref = enc.at[t, frm]
        if d:
            arrived(ref, bank_send.at[0], bank_recv.at[frm])
        for n, other in enumerate((tx, ty)):
            copy = remote(ref, ref, near_send.at[n, frm], near_recv.at[n, frm], tensor=other)
            copy.start()
            near_copies.append(copy)

    for c, b, other in ((0, tx, ty), (1, ty, tx)):
        ref = tok.at[b, pl.ds(c * half, half)]
        arrived(ref, tok_send.at[4 + c], tok_recv.at[2 * c + c])
        copy = remote(ref, ref, tok_send.at[4 + c], tok_recv.at[4 + c], tensor=other)
        copy.start()
        tok_copies.append(copy)

    pass_on(1)
    loads[2].wait()
    loads[3].wait()
    make_kv(t)
    arrived(tok.at[tx, pl.ds(half, half)], tok_send.at[0], tok_recv.at[1])
    wq_loads[1].wait()
    add_queries(tx, False)
    arrived(tok.at[ty, pl.ds(0, half)], tok_send.at[0], tok_recv.at[2])
    wq_loads[2].wait()
    add_queries(ty, False)

    for i in range(0, mem_count, 2):
        for n, b, other in ((0, tx, ty), (1, ty, tx)):
            ref = enc.at[b, i + n]
            arrived(ref, near_send.at[2, i + n], near_recv.at[n, i + n])
            copy = remote(ref, ref, near_send.at[2, i + n], near_recv.at[2, i + n], tensor=other)
            copy.start()
            near_copies.append(copy)
    if z_count > 2:
        pass_on(2)
    for i in range(1, mem_count, 2):
        arrived(enc.at[tx, i], near_send.at[0, 0], near_recv.at[0, i])
    make_kv(tx)
    for i in range(0, mem_count, 2):
        arrived(enc.at[ty, i], near_send.at[0, 0], near_recv.at[1, i])
    make_kv(ty)
    arrived(tok.at[td, pl.ds(0, half)], tok_send.at[0], tok_recv.at[4])
    arrived(tok.at[td, pl.ds(half, half)], tok_send.at[0], tok_recv.at[5])
    wq_loads[3].wait()
    add_queries(td, False)
    queries[...] = (acc[...] * score_scale).astype(jnp.bfloat16)
    for i in range(mem_count):
        arrived(enc.at[td, i], near_send.at[0, 0], near_recv.at[2, i])
    make_kv(td)

    span_rows = rows // spans

    def attend(stage):
        @pl.loop(stage * spans // 2, (stage + 1) * spans // 2)
        def _(c):
            first = source[NB * c]
            second = source[NB * c + 1]
            where = pl.ds(pl.multiple_of(c * span_rows, span_rows), span_rows)
            for h in range(width // DH):
                cols = slice(h * DH, (h + 1) * DH)
                k = jnp.concatenate(
                    [keys[b, s, :, cols] for s in (first, second) for b in range(tensor_count)], axis=0
                )
                v = jnp.concatenate(
                    [values[b, s, :, cols] for s in (first, second) for b in range(tensor_count)], axis=0
                )
                scores = lax.dot_general(
                    queries[where, cols], k, (((1,), (1,)), ((), ())), preferred_element_type=jnp.float32
                )
                lifted = jnp.exp(scores - jnp.max(scores, axis=-1, keepdims=True))
                weights = (lifted * (1.0 / jnp.sum(lifted, axis=-1, keepdims=True))).astype(jnp.bfloat16)
                attended[where, cols] = jnp.dot(weights, v, preferred_element_type=jnp.float32).astype(jnp.bfloat16)

    wide = wo.shape[2]
    quarter = half // 2

    def project(b, lo, out, extra=None, count=quarter):
        @pl.loop(0, 2)
        def _(j):
            @pl.loop(0, wide // tile)
            def _(n):
                inner = pl.ds(pl.multiple_of(n * tile, tile), tile)
                outer = pl.ds(pl.multiple_of(j * wide + n * tile, tile), tile)
                term = jnp.dot(
                    attended[lo : lo + count], wo[b * 2 + j, :, inner], preferred_element_type=jnp.float32
                ).astype(jnp.bfloat16)
                if extra is not None:
                    term = (term.astype(jnp.float32) + extra[:, outer].astype(jnp.float32)).astype(jnp.bfloat16)
                out[lo : lo + count, outer] = term

    def give(ref, dst, stage, i, other):
        remote(ref, dst, red_send.at[stage, i], red_recv.at[stage, i], tensor=other).start()

    def need(b, stage):
        if stage == 0:
            arrived(wo.at[2 * b + 1 - core], core_send.at[0], core_recv.at[b])

    def far():
        for s in range(3, z_count):
            pass_on(s)

    def places(stage):
        lo = stage * half
        return lo, lo + quarter, pl.ds(lo, quarter), pl.ds(lo + quarter, quarter), pl.ds(stage * quarter, quarter)

    def plain_x(stage):
        lo, hi, low, high, relay = places(stage)
        need(tx, stage)
        project(tx, lo, part_x)
        give(part_x.at[low], got_x.at[low], stage, 2, tx)

    def plain_y(stage):
        lo, hi, low, high, relay = places(stage)
        need(ty, stage)
        project(ty, hi, part_y)
        give(part_y.at[high], got_y.at[high], stage, 3, ty)

    def diagonal(stage):
        lo, hi, low, high, relay = places(stage)
        need(td, stage)
        project(td, lo, part_d)
        give(part_d.at[low], relay_x.at[relay], stage, 0, tx)
        project(td, hi, part_d)
        give(part_d.at[high], relay_y.at[relay], stage, 1, ty)

    def relayed(stage):
        lo, hi, low, high, relay = places(stage)
        arrived(relay_x.at[relay], red_send.at[0, 0], red_recv.at[stage, 0])
        project(ty, lo, part_y, relay_x.at[relay])
        give(part_y.at[low], got_y.at[low], stage, 4, ty)
        arrived(relay_y.at[relay], red_send.at[0, 0], red_recv.at[stage, 1])
        project(tx, hi, part_x, relay_y.at[relay])
        give(part_x.at[high], got_x.at[high], stage, 5, tx)

    attend(0)
    loads[4].wait()
    at_end = (z == 0) | (z == z_count - 1)
    last = z_count - 1 - z
    x_late = at_end & (tx == last)
    y_late = at_end & (ty == last)
    d_late = at_end & (td == last)

    @pl.when(x_late)
    def _():
        plain_y(0)
        diagonal(0)
        far()
        plain_x(0)

    @pl.when(y_late)
    def _():
        plain_x(0)
        diagonal(0)
        far()
        plain_y(0)

    @pl.when(d_late)
    def _():
        plain_x(0)
        plain_y(0)
        far()
        diagonal(0)

    @pl.when(jnp.logical_not(x_late | y_late | d_late))
    def _():
        plain_x(0)
        plain_y(0)
        diagonal(0)
        far()

    attend(1)
    plain_x(1)
    plain_y(1)
    diagonal(1)
    relayed(0)
    relayed(1)
    need(t, 0)
    for stage in range(2):
        lo, hi, low, high, relay = places(stage)
        left(part_d.at[low], red_send.at[stage, 0], red_recv.at[0, 0])
        left(part_d.at[high], red_send.at[stage, 1], red_recv.at[0, 0])
    project(t, 0, part_d, count=rows)
    for stage in range(2):
        lo, hi, low, high, relay = places(stage)
        for i, ref in ((2, got_x.at[low]), (3, got_y.at[high]), (4, got_y.at[low]), (5, got_x.at[high])):
            arrived(ref, red_send.at[0, 0], red_recv.at[stage, i])
        where = pl.ds(lo, half)
        result[where] = (
            part_d[where].astype(jnp.float32) + got_x[where].astype(jnp.float32) + got_y[where].astype(jnp.float32)
        ).astype(jnp.bfloat16)
        for i in range(2, 6):
            left(part_x.at[low], red_send.at[stage, i], red_recv.at[0, 0])

    for copy in bank_copies + tok_copies + near_copies:
        copy.wait_send()
    for s in range(z_count - 1):
        @pl.when((z < z_count - 1) & (z >= s))
        def _():
            left(wo.at[0], wo_send.at[0, s], wo_recv.at[0, 0])

        @pl.when((z > 0) & (z + s < z_count))
        def _():
            left(wo.at[0], wo_send.at[1, s], wo_recv.at[0, 0])
    for i in range(z_count):
        left(wo.at[0], core_send.at[i], core_recv.at[0])


def fused_body(tokens, neighbours, memory_bank, w_query, w_key, w_value, w_out):
    mem_count = lax.axis_size("mem")
    tensor_count = lax.axis_size("tensor")
    mem_index = lax.axis_index("mem")
    slice_len, enc_width = memory_bank.shape[1:]
    requests = neighbours.shape[0] * neighbours.shape[1] // mem_count
    spans = requests // NB
    slot_count = requests // mem_count
    rows, width = tokens.shape
    listing = neighbours.reshape(mem_count, requests, 2)
    owner_ids = listing[:, :, 0]
    row_ids = listing[:, :, 1]
    owned_here = owner_ids == mem_index
    slot_rank = jnp.cumsum(owned_here.astype(jnp.int32), axis=1) - 1
    slot_ids = jnp.arange(slot_count, dtype=jnp.int32)
    chosen = owned_here[:, None, :] & (slot_rank[:, None, :] == slot_ids[None, :, None])
    wanted = jnp.sum(jnp.where(chosen, row_ids[:, None, :], 0), axis=2)
    outgoing = jnp.take(memory_bank, wanted.reshape(-1), axis=0, mode="clip").reshape(
        mem_count, slot_count * slice_len, enc_width
    )
    own_owner = lax.dynamic_index_in_dim(listing, mem_index, 0, keepdims=False)[:, 0]
    positions = jnp.arange(requests, dtype=jnp.int32)
    earlier = positions[None, :] < positions[:, None]
    same_owner = own_owner[:, None] == own_owner[None, :]
    own_rank = jnp.sum((same_owner & earlier).astype(jnp.int32), axis=1)
    source = own_owner * slot_count + own_rank
    z_count = mem_count // 2
    bf16 = jnp.bfloat16
    half = rows // 2
    slots = mem_count * slot_count
    hbm = pl.BlockSpec(memory_space=pl.ANY)
    dma = pltpu.SemaphoreType.DMA
    return pl.pallas_call(
        functools.partial(fused_kernel, mem_count, tensor_count, spans, 1.0 / math.sqrt(DH)),
        out_shape=jax.ShapeDtypeStruct((rows, width), bf16),
        in_specs=[pl.BlockSpec(memory_space=pltpu.SMEM)] + [hbm] * 6,
        out_specs=pl.BlockSpec(memory_space=pltpu.VMEM),
        scratch_shapes=[
            pltpu.VMEM((tensor_count, rows, width), bf16),
            pltpu.VMEM((tensor_count, width, width), bf16),
            pltpu.VMEM((enc_width, width), bf16),
            pltpu.VMEM((enc_width, width), bf16),
            pltpu.VMEM((tensor_count, mem_count, slot_count * slice_len, enc_width), bf16),
            pltpu.VMEM((tensor_count, slots, slice_len, width), bf16),
            pltpu.VMEM((tensor_count, slots, slice_len, width), bf16),
            pltpu.VMEM((rows, width), jnp.float32),
            pltpu.VMEM((rows, width), bf16),
            pltpu.VMEM((rows, width), bf16),
            pltpu.VMEM((mem_count,) + w_out.shape, bf16),
            pltpu.VMEM((rows, width), bf16),
            pltpu.VMEM((rows, width), bf16),
            pltpu.VMEM((rows, width), bf16),
            pltpu.VMEM((half, width), bf16),
            pltpu.VMEM((half, width), bf16),
            pltpu.VMEM((rows, width), bf16),
            pltpu.VMEM((rows, width), bf16),
            dma((9,)),
            dma((6,)),
            dma((6,)),
            dma((mem_count,)),
            dma((mem_count,)),
            dma((3, mem_count)),
            dma((3, mem_count)),
            dma((2, z_count)),
            dma((2, z_count)),
            dma((z_count,)),
            dma((z_count,)),
            dma((2, 6)),
            dma((2, 6)),
        ],
        compiler_params=pltpu.CompilerParams(
            collective_id=0, has_side_effects=True, vmem_limit_bytes=58 * 1024 * 1024
        ),
    )(source, tokens, outgoing, w_query.reshape(tensor_count, width, width), w_key, w_value, w_out)


def fits(mesh, tokens, neighbours, memory_bank, w_query):
    mem_count, tensor_count = mesh.shape["mem"], mesh.shape["tensor"]
    requests = neighbours.shape[0] * neighbours.shape[1] // mem_count
    return (
        tensor_count == 4
        and mem_count == 2 * tensor_count
        and requests == NB * mem_count
        and tokens.shape[1] == w_query.shape[1]
    )


def solution(mesh):
    def run(*args):
        chosen = fused_body if fits(mesh, *args[:4]) else body
        return jax.shard_map(
            chosen,
            mesh=mesh,
            in_specs=(
                P("mem", "tensor"),
                P(),
                P("mem", "tensor", None),
                P(None, "tensor"),
                P(None, "tensor"),
                P(None, "tensor"),
                P("tensor", "mem"),
            ),
            out_specs=P("mem", "tensor"),
            check_vma=False,
        )(*args)

    return run
```

```python
import functools
import math

import jax
import jax.numpy as jnp
from jax import lax
from jax.experimental import pallas as pl
from jax.experimental.pallas import tpu as pltpu
from jax.sharding import PartitionSpec as P

DH = 128
NB = 2


def body(tokens, neighbours, memory_bank, w_query, w_key, w_value, w_out):
    mem_count = lax.axis_size("mem")
    mem_index = lax.axis_index("mem")
    slice_len = memory_bank.shape[1]
    enc_width = memory_bank.shape[2]
    head_cols = w_query.shape[1]
    heads_here = head_cols // DH
    requests = neighbours.shape[0] * neighbours.shape[1] // mem_count
    spans_here = requests // NB
    slot_count = max(2, (requests + mem_count - 1) // mem_count)
    score_scale = 1.0 / math.sqrt(DH)
    query_sum = jnp.dot(
        lax.all_gather(tokens, "tensor", axis=1, tiled=True),
        w_query,
        preferred_element_type=jnp.float32,
    )
    queries = (query_sum * score_scale).astype(jnp.bfloat16)
    listing = neighbours.reshape(mem_count, requests, 2)
    owner_ids = listing[:, :, 0]
    row_ids = listing[:, :, 1]
    owned_here = owner_ids == mem_index
    slot_rank = jnp.cumsum(owned_here.astype(jnp.int32), axis=1) - 1
    slot_ids = jnp.arange(slot_count, dtype=jnp.int32)
    chosen = owned_here[:, None, :] & (slot_rank[:, None, :] == slot_ids[None, :, None])
    wanted = jnp.sum(jnp.where(chosen, row_ids[:, None, :], 0), axis=2)
    outgoing = jnp.take(memory_bank, wanted.reshape(-1), axis=0).reshape(
        mem_count, slot_count, slice_len, enc_width
    )
    incoming = lax.all_to_all(outgoing, "mem", split_axis=0, concat_axis=0, tiled=True)
    own_list = lax.dynamic_index_in_dim(listing, mem_index, 0, keepdims=False)
    own_owner = own_list[:, 0]
    positions = jnp.arange(requests, dtype=jnp.int32)
    earlier = positions[None, :] < positions[:, None]
    same_owner = own_owner[:, None] == own_owner[None, :]
    own_rank = jnp.sum((same_owner & earlier).astype(jnp.int32), axis=1)
    source = own_owner * slot_count + own_rank
    fetched = jnp.take(
        incoming.reshape(mem_count * slot_count, slice_len, enc_width), source, axis=0
    )
    joined = jnp.concatenate([w_key, w_value], axis=1)
    key_value = jnp.dot(
        lax.all_gather(fetched, "tensor", axis=1, tiled=True),
        joined,
        preferred_element_type=jnp.float32,
    ).astype(jnp.bfloat16)
    bank_len = key_value.shape[1]
    key_block = key_value[:, :, :head_cols].reshape(spans_here, NB * bank_len, heads_here, DH)
    value_block = key_value[:, :, head_cols:].reshape(spans_here, NB * bank_len, heads_here, DH)
    query_block = queries.reshape(spans_here, -1, heads_here, DH)
    scores = jnp.einsum(
        "cqhd,ckhd->chqk", query_block, key_block, preferred_element_type=jnp.float32
    )
    row_max = jnp.max(scores, axis=-1, keepdims=True)
    lifted = jnp.exp(scores - row_max)
    normed = lifted / jnp.sum(lifted, axis=-1, keepdims=True)
    weights = normed.astype(jnp.bfloat16)
    attended = jnp.einsum(
        "chqk,ckhd->cqhd", weights, value_block, preferred_element_type=jnp.float32
    )
    attended = attended.astype(jnp.bfloat16).reshape(-1, head_cols)
    partial_value = jnp.dot(
        attended,
        lax.all_gather(w_out, "mem", axis=1, tiled=True),
        preferred_element_type=jnp.float32,
    )
    summed = lax.psum_scatter(
        partial_value.astype(jnp.bfloat16), "tensor", scatter_dimension=1, tiled=True
    )
    return summed


MESH = pl.DeviceIdType.MESH


def fused_kernel(
    mem_count, tensor_count, spans, score_scale,
    source, tokens, outgoing, w_query, w_key, w_value, w_out, result,
    tok, wq, wk, wv, enc, keys, values, acc, queries, attended, wo,
    part_d, part_x, part_y, relay_x, relay_y, got_x, got_y,
    load_sem, tok_send, tok_recv, bank_send, bank_recv, near_send, near_recv,
    wo_send, wo_recv, core_send, core_recv, red_send, red_recv,
):
    me = lax.axis_index("mem")
    t = lax.axis_index("tensor")
    tx = t + 1 - 2 * (t % 2)
    ty = (t + 2) % 4
    td = (tx + 2) % 4
    z_count = mem_count // 2
    z = me // 2
    core = me % 2
    mate = me + 1 - 2 * core
    rows = tok.shape[1]
    half = rows // 2
    width = tok.shape[2]
    tile = 256

    def remote(src, dst, send, recv, **where):
        return pltpu.make_async_remote_copy(
            src_ref=src, dst_ref=dst, send_sem=send, recv_sem=recv,
            device_id=where, device_id_type=MESH,
        )

    def arrived(ref, send, recv):
        remote(ref, ref, send, recv, tensor=tx).wait_recv()

    def left(ref, send, recv):
        remote(ref, ref, send, recv, tensor=tx).wait_send()

    barrier = pltpu.get_barrier_semaphore()
    for d in range(1, mem_count):
        pl.semaphore_signal(barrier, inc=1, device_id={"mem": (me + d) % mem_count}, device_id_type=MESH)
    for other in (tx, ty):
        pl.semaphore_signal(barrier, inc=1, device_id={"tensor": other}, device_id_type=MESH)

    loads = [
        pltpu.make_async_copy(tokens, tok.at[t], load_sem.at[0]),
        pltpu.make_async_copy(outgoing.at[me], enc.at[t, me], load_sem.at[1]),
        pltpu.make_async_copy(w_key, wk, load_sem.at[2]),
        pltpu.make_async_copy(w_value, wv, load_sem.at[3]),
        pltpu.make_async_copy(w_out, wo.at[me], load_sem.at[4]),
    ]
    wq_loads = []
    for i, b in enumerate((t, tx, ty, td)):
        wq_loads.append(pltpu.make_async_copy(w_query.at[b], wq.at[b], load_sem.at[5 + i]))
    for copy in loads[:2] + wq_loads + loads[2:]:
        copy.start()
    pl.semaphore_wait(barrier, mem_count + 1)

    bank_copies = []
    for d in range(1, mem_count):
        to = (me + d) % mem_count
        copy = remote(outgoing.at[to], enc.at[t, me], bank_send.at[d], bank_recv.at[me], mem=to)
        copy.start()
        bank_copies.append(copy)

    tok_copies = []
    for c in range(2):
        part = pl.ds(c * half, half)
        for n, other in enumerate((tx, ty)):
            copy = remote(
                tokens.at[part], tok.at[t, part], tok_send.at[2 * n + c], tok_recv.at[2 * n + c], tensor=other
            )
            copy.start()
            tok_copies.append(copy)

    def pass_on(s):
        @pl.when(z >= s)
        def _():
            ref = wo.at[me - 2 * s]
            arrived(ref, wo_send.at[0, s], wo_recv.at[0, s])
            remote(ref, ref, core_send.at[z - s], core_recv.at[z - s], mem=mate).start()
            if s < z_count - 1:
                @pl.when(z < z_count - 1)
                def _():
                    remote(ref, ref, wo_send.at[0, s], wo_recv.at[0, s + 1], mem=me + 2).start()

        @pl.when(z + s < z_count)
        def _():
            ref = wo.at[me + 2 * s]
            arrived(ref, wo_send.at[1, s], wo_recv.at[1, s])
            remote(ref, ref, core_send.at[z + s], core_recv.at[z + s], mem=mate).start()
            if s < z_count - 1:
                @pl.when(z > 0)
                def _():
                    remote(ref, ref, wo_send.at[1, s], wo_recv.at[1, s + 1], mem=me - 2).start()

    def add_queries(b, first):
        @pl.loop(0, width // tile)
        def _(n):
            cols = pl.ds(pl.multiple_of(n * tile, tile), tile)
            term = jnp.dot(tok[b], wq[b, :, cols], preferred_element_type=jnp.float32)
            if first:
                acc[:, cols] = term
            else:
                acc[:, cols] += term

    enc_rows = enc.shape[1] * enc.shape[2]
    enc_width = enc.shape[3]
    slots = keys.shape[1]
    length = keys.shape[2]

    def make_kv(b):
        @pl.loop(0, width // tile)
        def _(n):
            cols = pl.ds(pl.multiple_of(n * tile, tile), tile)
            block = enc[b].reshape(enc_rows, enc_width)
            k = jnp.dot(block, wk[:, cols], preferred_element_type=jnp.float32)
            keys[b, :, :, cols] = k.astype(jnp.bfloat16).reshape(slots, length, tile)
            v = jnp.dot(block, wv[:, cols], preferred_element_type=jnp.float32)
            values[b, :, :, cols] = v.astype(jnp.bfloat16).reshape(slots, length, tile)

    loads[0].wait()
    wq_loads[0].wait()
    add_queries(t, True)

    near_copies = []
    loads[1].wait()
    order = [0] + [d for k in range(1, mem_count // 2 + 1) for d in sorted({k, mem_count - k})]
    for d in order:
        frm = (me + d) % mem_count
        ref = enc.at[t, frm]
        if d:
            arrived(ref, bank_send.at[0], bank_recv.at[frm])
        for n, other in enumerate((tx, ty)):
            copy = remote(ref, ref, near_send.at[n, frm], near_recv.at[n, frm], tensor=other)
            copy.start()
            near_copies.append(copy)

    @pl.when(z < z_count - 1)
    def _():
        remote(w_out, wo.at[me], wo_send.at[0, 0], wo_recv.at[0, 1], mem=me + 2).start()

    @pl.when(z > 0)
    def _():
        remote(w_out, wo.at[me], wo_send.at[1, 0], wo_recv.at[1, 1], mem=me - 2).start()

    remote(w_out, wo.at[me], core_send.at[z], core_recv.at[z], mem=mate).start()

    for c, b, other in ((0, tx, ty), (1, ty, tx)):
        ref = tok.at[b, pl.ds(c * half, half)]
        arrived(ref, tok_send.at[4 + c], tok_recv.at[2 * c + c])
        copy = remote(ref, ref, tok_send.at[4 + c], tok_recv.at[4 + c], tensor=other)
        copy.start()
        tok_copies.append(copy)

    pass_on(1)
    loads[2].wait()
    loads[3].wait()
    make_kv(t)
    arrived(tok.at[tx, pl.ds(half, half)], tok_send.at[0], tok_recv.at[1])
    wq_loads[1].wait()
    add_queries(tx, False)
    arrived(tok.at[ty, pl.ds(0, half)], tok_send.at[0], tok_recv.at[2])
    wq_loads[2].wait()
    add_queries(ty, False)

    for i in range(0, mem_count, 2):
        for n, b, other in ((0, tx, ty), (1, ty, tx)):
            ref = enc.at[b, i + n]
            arrived(ref, near_send.at[2, i + n], near_recv.at[n, i + n])
            copy = remote(ref, ref, near_send.at[2, i + n], near_recv.at[2, i + n], tensor=other)
            copy.start()
            near_copies.append(copy)
    if z_count > 2:
        pass_on(2)
    for i in range(1, mem_count, 2):
        arrived(enc.at[tx, i], near_send.at[0, 0], near_recv.at[0, i])
    make_kv(tx)
    for i in range(0, mem_count, 2):
        arrived(enc.at[ty, i], near_send.at[0, 0], near_recv.at[1, i])
    make_kv(ty)
    arrived(tok.at[td, pl.ds(0, half)], tok_send.at[0], tok_recv.at[4])
    arrived(tok.at[td, pl.ds(half, half)], tok_send.at[0], tok_recv.at[5])
    wq_loads[3].wait()
    add_queries(td, False)
    queries[...] = (acc[...] * score_scale).astype(jnp.bfloat16)
    for i in range(mem_count):
        arrived(enc.at[td, i], near_send.at[0, 0], near_recv.at[2, i])
    make_kv(td)

    span_rows = rows // spans

    def attend(stage):
        @pl.loop(stage * spans // 2, (stage + 1) * spans // 2)
        def _(c):
            first = source[NB * c]
            second = source[NB * c + 1]
            where = pl.ds(pl.multiple_of(c * span_rows, span_rows), span_rows)
            for h in range(width // DH):
                cols = slice(h * DH, (h + 1) * DH)
                k = jnp.concatenate(
                    [keys[b, s, :, cols] for s in (first, second) for b in range(tensor_count)], axis=0
                )
                v = jnp.concatenate(
                    [values[b, s, :, cols] for s in (first, second) for b in range(tensor_count)], axis=0
                )
                scores = lax.dot_general(
                    queries[where, cols], k, (((1,), (1,)), ((), ())), preferred_element_type=jnp.float32
                )
                lifted = jnp.exp(scores - jnp.max(scores, axis=-1, keepdims=True))
                weights = (lifted * (1.0 / jnp.sum(lifted, axis=-1, keepdims=True))).astype(jnp.bfloat16)
                attended[where, cols] = jnp.dot(weights, v, preferred_element_type=jnp.float32).astype(jnp.bfloat16)

    wide = wo.shape[2]
    quarter = half // 2

    def project(b, lo, out, extra=None, count=quarter):
        @pl.loop(0, 2)
        def _(j):
            @pl.loop(0, wide // tile)
            def _(n):
                inner = pl.ds(pl.multiple_of(n * tile, tile), tile)
                outer = pl.ds(pl.multiple_of(j * wide + n * tile, tile), tile)
                term = jnp.dot(
                    attended[lo : lo + count], wo[b * 2 + j, :, inner], preferred_element_type=jnp.float32
                ).astype(jnp.bfloat16)
                if extra is not None:
                    term = (term.astype(jnp.float32) + extra[:, outer].astype(jnp.float32)).astype(jnp.bfloat16)
                out[lo : lo + count, outer] = term

    def give(ref, dst, stage, i, other):
        remote(ref, dst, red_send.at[stage, i], red_recv.at[stage, i], tensor=other).start()

    def need(b, stage):
        if stage == 0:
            arrived(wo.at[2 * b + 1 - core], core_send.at[0], core_recv.at[b])

    def far():
        for s in range(3, z_count):
            pass_on(s)

    def places(stage):
        lo = stage * half
        return lo, lo + quarter, pl.ds(lo, quarter), pl.ds(lo + quarter, quarter), pl.ds(stage * quarter, quarter)

    def plain_x(stage):
        lo, hi, low, high, relay = places(stage)
        need(tx, stage)
        project(tx, lo, part_x)
        give(part_x.at[low], got_x.at[low], stage, 2, tx)

    def plain_y(stage):
        lo, hi, low, high, relay = places(stage)
        need(ty, stage)
        project(ty, hi, part_y)
        give(part_y.at[high], got_y.at[high], stage, 3, ty)

    def diagonal(stage):
        lo, hi, low, high, relay = places(stage)
        need(td, stage)
        project(td, lo, part_d)
        give(part_d.at[low], relay_x.at[relay], stage, 0, tx)
        project(td, hi, part_d)
        give(part_d.at[high], relay_y.at[relay], stage, 1, ty)

    def relayed(stage):
        lo, hi, low, high, relay = places(stage)
        arrived(relay_x.at[relay], red_send.at[0, 0], red_recv.at[stage, 0])
        project(ty, lo, part_y, relay_x.at[relay])
        give(part_y.at[low], got_y.at[low], stage, 4, ty)
        arrived(relay_y.at[relay], red_send.at[0, 0], red_recv.at[stage, 1])
        project(tx, hi, part_x, relay_y.at[relay])
        give(part_x.at[high], got_x.at[high], stage, 5, tx)

    attend(0)
    loads[4].wait()
    at_end = (z == 0) | (z == z_count - 1)
    last = z_count - 1 - z
    x_late = at_end & (tx == last)
    y_late = at_end & (ty == last)
    d_late = at_end & (td == last)

    @pl.when(x_late)
    def _():
        plain_y(0)
        diagonal(0)
        far()
        plain_x(0)

    @pl.when(y_late)
    def _():
        plain_x(0)
        diagonal(0)
        far()
        plain_y(0)

    @pl.when(d_late)
    def _():
        plain_x(0)
        plain_y(0)
        far()
        diagonal(0)

    @pl.when(jnp.logical_not(x_late | y_late | d_late))
    def _():
        plain_x(0)
        plain_y(0)
        diagonal(0)
        far()

    attend(1)
    plain_x(1)
    plain_y(1)
    diagonal(1)
    relayed(0)
    relayed(1)
    need(t, 0)
    for stage in range(2):
        lo, hi, low, high, relay = places(stage)
        left(part_d.at[low], red_send.at[stage, 0], red_recv.at[0, 0])
        left(part_d.at[high], red_send.at[stage, 1], red_recv.at[0, 0])
    project(t, 0, part_d, count=rows)
    for stage in range(2):
        lo, hi, low, high, relay = places(stage)
        for i, ref in ((2, got_x.at[low]), (3, got_y.at[high]), (4, got_y.at[low]), (5, got_x.at[high])):
            arrived(ref, red_send.at[0, 0], red_recv.at[stage, i])
        where = pl.ds(lo, half)
        result[where] = (
            part_d[where].astype(jnp.float32) + got_x[where].astype(jnp.float32) + got_y[where].astype(jnp.float32)
        ).astype(jnp.bfloat16)
        for i in range(2, 6):
            left(part_x.at[low], red_send.at[stage, i], red_recv.at[0, 0])

    for copy in bank_copies + tok_copies + near_copies:
        copy.wait_send()
    for s in range(z_count - 1):
        @pl.when((z < z_count - 1) & (z >= s))
        def _():
            left(wo.at[0], wo_send.at[0, s], wo_recv.at[0, 0])

        @pl.when((z > 0) & (z + s < z_count))
        def _():
            left(wo.at[0], wo_send.at[1, s], wo_recv.at[0, 0])
    for i in range(z_count):
        left(wo.at[0], core_send.at[i], core_recv.at[0])


def fused_body(tokens, neighbours, memory_bank, w_query, w_key, w_value, w_out):
    mem_count = lax.axis_size("mem")
    tensor_count = lax.axis_size("tensor")
    mem_index = lax.axis_index("mem")
    slice_len, enc_width = memory_bank.shape[1:]
    requests = neighbours.shape[0] * neighbours.shape[1] // mem_count
    spans = requests // NB
    slot_count = requests // mem_count
    rows, width = tokens.shape
    listing = neighbours.reshape(mem_count, requests, 2)
    owner_ids = listing[:, :, 0]
    row_ids = listing[:, :, 1]
    owned_here = owner_ids == mem_index
    slot_rank = jnp.cumsum(owned_here.astype(jnp.int32), axis=1) - 1
    slot_ids = jnp.arange(slot_count, dtype=jnp.int32)
    chosen = owned_here[:, None, :] & (slot_rank[:, None, :] == slot_ids[None, :, None])
    wanted = jnp.sum(jnp.where(chosen, row_ids[:, None, :], 0), axis=2)
    outgoing = jnp.take(memory_bank, wanted.reshape(-1), axis=0, mode="clip").reshape(
        mem_count, slot_count * slice_len, enc_width
    )
    own_owner = lax.dynamic_index_in_dim(listing, mem_index, 0, keepdims=False)[:, 0]
    positions = jnp.arange(requests, dtype=jnp.int32)
    earlier = positions[None, :] < positions[:, None]
    same_owner = own_owner[:, None] == own_owner[None, :]
    own_rank = jnp.sum((same_owner & earlier).astype(jnp.int32), axis=1)
    source = own_owner * slot_count + own_rank
    z_count = mem_count // 2
    bf16 = jnp.bfloat16
    half = rows // 2
    slots = mem_count * slot_count
    hbm = pl.BlockSpec(memory_space=pl.ANY)
    dma = pltpu.SemaphoreType.DMA
    return pl.pallas_call(
        functools.partial(fused_kernel, mem_count, tensor_count, spans, 1.0 / math.sqrt(DH)),
        out_shape=jax.ShapeDtypeStruct((rows, width), bf16),
        in_specs=[pl.BlockSpec(memory_space=pltpu.SMEM)] + [hbm] * 6,
        out_specs=pl.BlockSpec(memory_space=pltpu.VMEM),
        scratch_shapes=[
            pltpu.VMEM((tensor_count, rows, width), bf16),
            pltpu.VMEM((tensor_count, width, width), bf16),
            pltpu.VMEM((enc_width, width), bf16),
            pltpu.VMEM((enc_width, width), bf16),
            pltpu.VMEM((tensor_count, mem_count, slot_count * slice_len, enc_width), bf16),
            pltpu.VMEM((tensor_count, slots, slice_len, width), bf16),
            pltpu.VMEM((tensor_count, slots, slice_len, width), bf16),
            pltpu.VMEM((rows, width), jnp.float32),
            pltpu.VMEM((rows, width), bf16),
            pltpu.VMEM((rows, width), bf16),
            pltpu.VMEM((mem_count,) + w_out.shape, bf16),
            pltpu.VMEM((rows, width), bf16),
            pltpu.VMEM((rows, width), bf16),
            pltpu.VMEM((rows, width), bf16),
            pltpu.VMEM((half, width), bf16),
            pltpu.VMEM((half, width), bf16),
            pltpu.VMEM((rows, width), bf16),
            pltpu.VMEM((rows, width), bf16),
            dma((9,)),
            dma((6,)),
            dma((6,)),
            dma((mem_count,)),
            dma((mem_count,)),
            dma((3, mem_count)),
            dma((3, mem_count)),
            dma((2, z_count)),
            dma((2, z_count)),
            dma((z_count,)),
            dma((z_count,)),
            dma((2, 6)),
            dma((2, 6)),
        ],
        compiler_params=pltpu.CompilerParams(
            collective_id=0, has_side_effects=True, vmem_limit_bytes=58 * 1024 * 1024
        ),
    )(source, tokens, outgoing, w_query.reshape(tensor_count, width, width), w_key, w_value, w_out)


def fits(mesh, tokens, neighbours, memory_bank, w_query):
    mem_count, tensor_count = mesh.shape["mem"], mesh.shape["tensor"]
    requests = neighbours.shape[0] * neighbours.shape[1] // mem_count
    return (
        tensor_count == 4
        and mem_count == 2 * tensor_count
        and requests == NB * mem_count
        and tokens.shape[1] == w_query.shape[1]
    )


def solution(mesh):
    def run(*args):
        chosen = fused_body if fits(mesh, *args[:4]) else body
        return jax.shard_map(
            chosen,
            mesh=mesh,
            in_specs=(
                P("mem", "tensor"),
                P(),
                P("mem", "tensor", None),
                P(None, "tensor"),
                P(None, "tensor"),
                P(None, "tensor"),
                P("tensor", "mem"),
            ),
            out_specs=P("mem", "tensor"),
            check_vma=False,
        )(*args)

    return run
```
